32 devices in a mesh: lat: 8 (over z, x), lon: 4 (over y, core).
Axes of the slice: x: 2, y: 2, z: 4, core: 2. Of those that a mesh axis runs over, the one named last changes fastest.
Arguments:
- cotangent: bfloat16 [128, 1440, 256], P('lat', 'lon'), may hold values from -6 to 6
- legendre: bfloat16 [128, 384, 192], P('lat', 'lon'), may hold values from -0.5 to 0.5
- spectral_weight: bfloat16 [256, 256], replicated, may hold values from -0.375 to 0.375
- skip_weight: bfloat16 [256, 256], replicated, may hold values from -0.375 to 0.375
Outputs:
- grad_input: bfloat16 [128, 1440, 256], P('lat', 'lon')
The draws below stay inside these ranges and needn't reach their ends.
All inputs are finite; a program needn't handle non-finite values.
Results may differ from the reference program's by a relative error of at most 0.015.
Values may be sent and summed in bfloat16 or wider, within the bound.
A program may use at most 128 MiB of HBM per device.

```python
import math
import jax
import jax.numpy as jnp
from jax import lax

C = 256
NLON = 1440
MM = 384
LH = 192
LAT_DEV = 16
NLAT = 128


def block_levels(own_key, extent, split, least, largest):
    loudness = 1.0
    for position, blocks in split:
        draws = jax.random.uniform(jax.random.fold_in(jax.random.fold_in(own_key, 6), position), (blocks,), jnp.float32, least / len(split), largest / len(split))
        loudness = loudness * jnp.repeat(jnp.exp(draws), extent[position] // blocks).reshape((-1,) + (1,) * (len(extent) - 1 - position))
    return loudness


def scatter_about(rng, dims, scale, bound, shards=(), kind=jnp.bfloat16):
    drawn = scale * jax.random.normal(rng, dims, jnp.float32)
    if shards:
        drawn = drawn * block_levels(rng, dims, shards, -0.22, 0.18)
    return jnp.clip(drawn, -bound, bound).astype(kind)


def setup_inputs(seed: int = 0) -> dict:
    key_of = jax.random.split(jax.random.key(seed), 5)
    return {
        "cotangent": scatter_about(key_of[0], (NLAT, NLON, C), 1.0, 6.0, ((0, 8), (1, 4))),
        "legendre": scatter_about(key_of[1], (NLAT, MM, LH), NLAT ** -0.5, 0.5, ((0, 8), (1, 4))),
        "spectral_weight": scatter_about(key_of[2], (C, C), C ** -0.5, 0.375),
        "skip_weight": scatter_about(key_of[3], (C, C), C ** -0.5, 0.375),
    }


def degree_masks(wave_start, wave_count, half_deg):
    wavenum = wave_start + lax.broadcasted_iota(jnp.int32, (wave_count, half_deg), 0)
    degree = 2 * lax.broadcasted_iota(jnp.int32, (wave_count, half_deg), 1)
    parity = wavenum % 2
    return (degree + parity >= wavenum, degree + 1 - parity >= wavenum)

def mix_channels(spectral, spectral_weight):
    width = spectral.shape[-1]
    flat_values = spectral.reshape(-1, width)
    mixed_out = jnp.dot(flat_values, spectral_weight.T, preferred_element_type=jnp.float32)
    return mixed_out.astype(jnp.bfloat16).reshape(spectral.shape)

def band_total(basis, values):
    band_count = basis.shape[0] // LAT_DEV
    basis_bands = basis.reshape((band_count, LAT_DEV) + basis.shape[1:])
    value_bands = values.reshape((band_count, LAT_DEV) + values.shape[1:])

    def advance(running, operands):
        contrib = jnp.einsum('rmk,rmpc->kmpc', operands[0].astype(jnp.float32), operands[1].astype(jnp.float32))
        contrib = lax.optimization_barrier(contrib.astype(jnp.bfloat16)).astype(jnp.float32)
        return (running + contrib, None)
    initial = jnp.zeros((basis.shape[2], basis.shape[1], 2, values.shape[-1]), jnp.float32)
    running, unused = lax.scan(advance, initial, (basis_bands, value_bands))
    return running

def reference(cotangent, legendre, spectral_weight, skip_weight):
    count_lat, count_lon, width = cotangent.shape
    count_wave = legendre.shape[1]
    half_deg = legendre.shape[2]
    half_rows = count_lat // 2
    norm_scale = math.sqrt(2.0 / count_lon)
    spectrum = jnp.fft.rfft(cotangent.astype(jnp.float32), axis=1)[:, :count_wave]
    coeffs = (norm_scale * jnp.stack([jnp.real(spectrum), jnp.imag(spectrum)], axis=2)).astype(jnp.bfloat16)
    mask_even, mask_odd = degree_masks(0, count_wave, half_deg)
    north_rows = legendre[:half_rows]
    south_rows = legendre[half_rows:]
    north_basis = jnp.where(mask_even[None], north_rows, jnp.zeros_like(north_rows))
    south_basis = jnp.where(mask_odd[None], south_rows, jnp.zeros_like(south_rows))
    north_wide = coeffs[:half_rows].astype(jnp.float32)
    south_wide = coeffs[half_rows:].astype(jnp.float32)
    comb_even = (north_wide + south_wide).astype(jnp.bfloat16)
    comb_odd = (north_wide - south_wide).astype(jnp.bfloat16)
    degree_split = jnp.stack([band_total(north_basis, comb_even), band_total(south_basis, comb_odd)]).astype(jnp.bfloat16)
    mixed_out = mix_channels(degree_split, spectral_weight)
    proj_even = jnp.einsum('rmk,kmpc->rmpc', north_basis.astype(jnp.float32), mixed_out[0].astype(jnp.float32))
    proj_even = lax.optimization_barrier(proj_even.astype(jnp.bfloat16)).astype(jnp.float32)
    proj_odd = jnp.einsum('rmk,kmpc->rmpc', south_basis.astype(jnp.float32), mixed_out[1].astype(jnp.float32))
    proj_odd = lax.optimization_barrier(proj_odd.astype(jnp.bfloat16)).astype(jnp.float32)
    grad_coeffs = jnp.concatenate([proj_even + proj_odd, proj_even - proj_odd], 0).astype(jnp.bfloat16)
    real_part = grad_coeffs[:, :, 0, :].astype(jnp.float32)
    imag_part = grad_coeffs[:, :, 1, :].astype(jnp.float32)
    padding = count_lon // 2 + 1 - count_wave
    spectral_full = lax.complex(jnp.pad(real_part, ((0, 0), (0, padding), (0, 0))), jnp.pad(imag_part, ((0, 0), (0, padding), (0, 0))))
    grid_part = norm_scale * (0.5 * count_lon * jnp.fft.irfft(spectral_full, n=count_lon, axis=1) + 0.5 * real_part[:, 0:1, :])
    grid_part = grid_part.astype(jnp.bfloat16)
    skip_term = jnp.dot(cotangent.reshape(-1, width), skip_weight.T, preferred_element_type=jnp.float32).reshape(cotangent.shape)
    return (grid_part.astype(jnp.float32) + skip_term).astype(jnp.bfloat16)
```

```python
import functools
import math

import jax
import jax.numpy as jnp
import numpy as np
from jax import lax
from jax.sharding import PartitionSpec as P

BOTH = ("lat", "lon")


def fourier_table(count_lon, count_wave, lat_count, lon_count, wave_each):
    wave_dev = count_wave // lon_count
    place = np.arange(lat_count * wave_each).reshape(lat_count, 1, wave_each)
    wavenum = place + wave_dev * np.arange(lon_count).reshape(1, lon_count, 1)
    real = np.broadcast_to(place < wave_dev, wavenum.shape)
    phases = wavenum[..., None] * np.arange(count_lon) % count_lon
    angles = phases * (2.0 * math.pi / count_lon)
    norm_scale = math.sqrt(2.0 / count_lon)
    table = np.stack([norm_scale * np.cos(angles), -norm_scale * np.sin(angles)], axis=2)
    table = np.where(real[:, :, None, :, None], table, 0.0)
    return table.reshape(-1, count_lon).astype(jnp.bfloat16)


def shards(table, cotangent, legendre, spectral_weight, skip_weight):
    lat_rows, lon_dev, width = cotangent.shape
    lat_count = lax.axis_size("lat")
    lon_count = lax.axis_size("lon")
    wave_dev, half_deg = legendre.shape[1:]
    wave_each = -(-wave_dev // lat_count)
    count_lat = lat_rows * lat_count
    half_rows = count_lat // 2
    fourier = jnp.asarray(table)

    rows = lax.all_to_all(cotangent, "lon", split_axis=0, concat_axis=1, tiled=True)
    padded = jnp.pad(legendre, ((0, 0), (0, wave_each * lat_count - wave_dev), (0, 0)))
    basis = lax.all_to_all(padded, "lat", split_axis=1, concat_axis=0, tiled=True)
    spectra = jnp.einsum(
        "kl,rlc->rkc", fourier, rows, preferred_element_type=jnp.float32
    ).astype(jnp.bfloat16)
    coeffs = lax.all_to_all(spectra, BOTH, split_axis=1, concat_axis=0, tiled=True)
    coeffs = coeffs.reshape(2, half_rows, 2, wave_each, width)

    wave_start = lax.axis_index("lon") * wave_dev + lax.axis_index("lat") * wave_each
    wavenum = wave_start + lax.broadcasted_iota(jnp.int32, (2, 1, wave_each, half_deg), 2)
    degree = 2 * lax.broadcasted_iota(jnp.int32, (2, 1, wave_each, half_deg), 3)
    half = lax.broadcasted_iota(jnp.int32, (2, 1, wave_each, half_deg), 0)
    parity = wavenum % 2
    degree = degree + jnp.where(half == 0, parity, 1 - parity)
    basis = basis.reshape(2, half_rows, wave_each, half_deg)
    basis = jnp.where(degree >= wavenum, basis, jnp.zeros_like(basis))

    wide = coeffs.astype(jnp.float32)
    combined = jnp.stack([wide[0] + wide[1], wide[0] - wide[1]]).astype(jnp.bfloat16)
    sums = jnp.einsum(
        "qrmk,qrpmc->qmkpc", basis, combined, preferred_element_type=jnp.float32
    ).astype(jnp.bfloat16)
    mixed = jnp.einsum(
        "qmkpc,dc->qmkpd", sums, spectral_weight, preferred_element_type=jnp.float32
    ).astype(jnp.bfloat16)
    projected = jnp.einsum(
        "qrmk,qmkpc->qrpmc", basis, mixed, preferred_element_type=jnp.float32
    ).astype(jnp.bfloat16).astype(jnp.float32)
    grads = jnp.stack([projected[0] + projected[1], projected[0] - projected[1]])
    grads = grads.astype(jnp.bfloat16).reshape(count_lat, 2 * wave_each, width)
    grads = lax.all_to_all(grads, BOTH, split_axis=0, concat_axis=1, tiled=True)
    grid_part = jnp.einsum(
        "kl,rkc->rlc", fourier, grads, preferred_element_type=jnp.float32
    ).astype(jnp.bfloat16)
    spatial = lax.all_to_all(grid_part, "lon", split_axis=1, concat_axis=0, tiled=True)
    skip_term = jnp.dot(
        cotangent.reshape(-1, width), skip_weight.T, preferred_element_type=jnp.float32
    ).reshape(cotangent.shape)
    return (spatial.astype(jnp.float32) + skip_term).astype(jnp.bfloat16)


def solution(mesh):
    lat_count, lon_count = mesh.shape["lat"], mesh.shape["lon"]

    def whole(cotangent, legendre, spectral_weight, skip_weight):
        count_wave = legendre.shape[1]
        wave_each = -(-(count_wave // lon_count) // lat_count)
        table = fourier_table(cotangent.shape[1], count_wave, lat_count, lon_count, wave_each)
        return jax.shard_map(
            functools.partial(shards, table),
            mesh=mesh,
            in_specs=(P("lat", "lon", None), P("lat", "lon", None), P(), P()),
            out_specs=P("lat", "lon", None),
            check_vma=False,
        )(cotangent, legendre, spectral_weight, skip_weight)

    return whole
```

```python
import functools
import math

import jax
import jax.numpy as jnp
import numpy as np
from jax import lax
from jax.experimental import pallas as pl
from jax.experimental.pallas import tpu as pltpu
from jax.sharding import PartitionSpec as P

BOTH = ("lat", "lon")


def fourier_table(count_lon, count_wave, lat_count, lon_count, wave_each):
    wave_dev = count_wave // lon_count
    place = np.arange(lat_count * wave_each).reshape(lat_count, 1, wave_each)
    wavenum = place + wave_dev * np.arange(lon_count).reshape(1, lon_count, 1)
    real = np.broadcast_to(place < wave_dev, wavenum.shape)
    phases = wavenum[..., None] * np.arange(count_lon) % count_lon
    angles = phases * (2.0 * math.pi / count_lon)
    norm_scale = math.sqrt(2.0 / count_lon)
    table = np.stack([norm_scale * np.cos(angles), -norm_scale * np.sin(angles)], axis=2)
    table = np.where(real[:, :, None, :, None], table, 0.0)
    return table.reshape(-1, count_lon).astype(jnp.bfloat16)


def exchange_kernel(
    lat_count, lon_count, cot_ref, leg_ref, rows_ref, basis_ref,
    cot_send, cot_recv, leg_send, leg_recv, own_sem,
):
    lat, lon = lax.axis_index("lat"), lax.axis_index("lon")
    barrier = pltpu.get_barrier_semaphore()
    partners = [(lat, lax.rem(lon + step, lon_count)) for step in range(1, lon_count)]
    partners += [(lax.rem(lat + step, lat_count), lon) for step in range(1, lat_count)]
    for partner in partners:
        pl.semaphore_signal(
            barrier, inc=1, device_id=partner, device_id_type=pl.DeviceIdType.MESH
        )
    pl.semaphore_wait(barrier, len(partners))
    copies = []
    for step in range(1, lon_count):
        there = lax.rem(lon + step, lon_count)
        copies.append(
            pltpu.make_async_remote_copy(
                src_ref=cot_ref.at[there],
                dst_ref=rows_ref.at[:, lon],
                send_sem=cot_send.at[step],
                recv_sem=cot_recv.at[step],
                device_id=(lat, there),
                device_id_type=pl.DeviceIdType.MESH,
            )
        )
    for step in range(1, lat_count):
        there = lax.rem(lat + step, lat_count)
        copies.append(
            pltpu.make_async_remote_copy(
                src_ref=leg_ref.at[there],
                dst_ref=basis_ref.at[lat],
                send_sem=leg_send.at[step],
                recv_sem=leg_recv.at[step],
                device_id=(there, lon),
                device_id_type=pl.DeviceIdType.MESH,
            )
        )
    copies.append(pltpu.make_async_copy(cot_ref.at[lon], rows_ref.at[:, lon], own_sem.at[0]))
    copies.append(pltpu.make_async_copy(leg_ref.at[lat], basis_ref.at[lat], own_sem.at[1]))
    for copy in copies:
        copy.start()
    for copy in copies:
        copy.wait()


def exchange(cotangent, basis, lat_count, lon_count):
    lat_rows, lon_dev, width = cotangent.shape
    rows_each = lat_rows // lon_count
    anywhere = pl.BlockSpec(memory_space=pl.ANY)
    return pl.pallas_call(
        functools.partial(exchange_kernel, lat_count, lon_count),
        out_shape=(
            jax.ShapeDtypeStruct((rows_each, lon_count, lon_dev, width), jnp.bfloat16),
            jax.ShapeDtypeStruct(basis.shape, jnp.bfloat16),
        ),
        in_specs=[anywhere] * 2,
        out_specs=(anywhere, anywhere),
        scratch_shapes=[
            pltpu.SemaphoreType.DMA((lon_count,)),
            pltpu.SemaphoreType.DMA((lon_count,)),
            pltpu.SemaphoreType.DMA((lat_count,)),
            pltpu.SemaphoreType.DMA((lat_count,)),
            pltpu.SemaphoreType.DMA((2,)),
        ],
        compiler_params=pltpu.CompilerParams(collective_id=0, has_side_effects=True),
    )(cotangent.reshape(lon_count, rows_each, lon_dev, width), basis)


def shards(table, cotangent, legendre, spectral_weight, skip_weight):
    lat_rows, lon_dev, width = cotangent.shape
    lat_count = lax.axis_size("lat")
    lon_count = lax.axis_size("lon")
    wave_dev, half_deg = legendre.shape[1:]
    wave_each = -(-wave_dev // lat_count)
    count_lat = lat_rows * lat_count
    half_rows = count_lat // 2
    fourier = jnp.asarray(table)

    padded = jnp.pad(legendre, ((0, 0), (0, wave_each * lat_count - wave_dev), (0, 0)))
    padded = padded.reshape(lat_rows, lat_count, wave_each, half_deg).transpose(1, 2, 0, 3)
    rows, basis = exchange(cotangent, padded, lat_count, lon_count)
    rows = rows.reshape(-1, lon_dev * lon_count, width)
    spectra = jnp.einsum(
        "kl,rlc->rkc", fourier, rows, preferred_element_type=jnp.float32
    ).astype(jnp.bfloat16)
    coeffs = lax.all_to_all(spectra, BOTH, split_axis=1, concat_axis=0, tiled=True)
    coeffs = coeffs.reshape(2, half_rows, 2, wave_each, width)

    wave_start = lax.axis_index("lon") * wave_dev + lax.axis_index("lat") * wave_each
    extent = (2, 1, wave_each, 1, half_deg)
    wavenum = wave_start + lax.broadcasted_iota(jnp.int32, extent, 2)
    degree = 2 * lax.broadcasted_iota(jnp.int32, extent, 4)
    half = lax.broadcasted_iota(jnp.int32, extent, 0)
    parity = wavenum % 2
    degree = degree + jnp.where(half == 0, parity, 1 - parity)
    basis = basis.reshape(2, lat_count // 2, wave_each, lat_rows, half_deg)
    basis = jnp.where(degree >= wavenum, basis, jnp.zeros_like(basis))
    basis = basis.transpose(0, 2, 1, 3, 4).reshape(2, wave_each, half_rows, half_deg)

    wide = coeffs.astype(jnp.float32)
    combined = jnp.stack([wide[0] + wide[1], wide[0] - wide[1]]).astype(jnp.bfloat16)
    sums = jnp.einsum(
        "qmrk,qrpmc->qmkpc", basis, combined, preferred_element_type=jnp.float32
    ).astype(jnp.bfloat16)
    mixed = jnp.einsum(
        "qmkpc,dc->qmkpd", sums, spectral_weight, preferred_element_type=jnp.float32
    ).astype(jnp.bfloat16)
    projected = jnp.einsum(
        "qmrk,qmkpc->qrpmc", basis, mixed, preferred_element_type=jnp.float32
    ).astype(jnp.bfloat16).astype(jnp.float32)
    grads = jnp.stack([projected[0] + projected[1], projected[0] - projected[1]])
    grads = grads.astype(jnp.bfloat16).reshape(count_lat, 2 * wave_each, width)
    grads = lax.all_to_all(grads, BOTH, split_axis=0, concat_axis=1, tiled=True)
    grid_part = jnp.einsum(
        "kl,rkc->rlc", fourier, grads, preferred_element_type=jnp.float32
    ).astype(jnp.bfloat16)
    grid_part = grid_part.reshape(-1, lon_count, lon_dev, width).transpose(1, 0, 2, 3)
    spatial = lax.all_to_all(grid_part, "lon", split_axis=0, concat_axis=0, tiled=True)
    spatial = spatial.reshape(cotangent.shape)
    skip_term = jnp.dot(
        cotangent.reshape(-1, width), skip_weight.T, preferred_element_type=jnp.float32
    ).reshape(cotangent.shape)
    return (spatial.astype(jnp.float32) + skip_term).astype(jnp.bfloat16)


def solution(mesh):
    lat_count, lon_count = mesh.shape["lat"], mesh.shape["lon"]

    def whole(cotangent, legendre, spectral_weight, skip_weight):
        count_wave = legendre.shape[1]
        wave_each = -(-(count_wave // lon_count) // lat_count)
        table = fourier_table(cotangent.shape[1], count_wave, lat_count, lon_count, wave_each)
        return jax.shard_map(
            functools.partial(shards, table),
            mesh=mesh,
            in_specs=(P("lat", "lon", None), P("lat", "lon", None), P(), P()),
            out_specs=P("lat", "lon", None),
            check_vma=False,
        )(cotangent, legendre, spectral_weight, skip_weight)

    return whole
```

```python
import functools
import math

import jax
import jax.numpy as jnp
import numpy as np
from jax import lax
from jax.experimental import pallas as pl
from jax.experimental.pallas import tpu as pltpu
from jax.sharding import PartitionSpec as P

BOTH = ("lat", "lon")


def fourier_table(count_lon, count_wave, lat_count, lon_count, wave_each):
    wave_dev = count_wave // lon_count
    place = np.arange(lat_count * wave_each).reshape(lat_count, 1, wave_each)
    wavenum = place + wave_dev * np.arange(lon_count).reshape(1, lon_count, 1)
    real = np.broadcast_to(place < wave_dev, wavenum.shape)
    phases = wavenum[..., None] * np.arange(count_lon) % count_lon
    angles = phases * (2.0 * math.pi / count_lon)
    norm_scale = math.sqrt(2.0 / count_lon)
    table = np.stack([norm_scale * np.cos(angles), -norm_scale * np.sin(angles)], axis=2)
    table = np.where(real[:, :, None, :, None], table, 0.0)
    return table.reshape(-1, count_lon).astype(jnp.bfloat16)


def exchange_kernel(
    lat_count, lon_count, cot_ref, leg_ref, rows_ref, basis_ref,
    cot_send, cot_recv, leg_send, leg_recv, own_sem,
):
    lat, lon = lax.axis_index("lat"), lax.axis_index("lon")
    barrier = pltpu.get_barrier_semaphore()
    partners = [(lat, lax.rem(lon + step, lon_count)) for step in range(1, lon_count)]
    partners += [(lax.rem(lat + step, lat_count), lon) for step in range(1, lat_count)]
    for partner in partners:
        pl.semaphore_signal(
            barrier, inc=1, device_id=partner, device_id_type=pl.DeviceIdType.MESH
        )
    pl.semaphore_wait(barrier, len(partners))
    copies = []
    for step in range(1, lon_count):
        there = lax.rem(lon + step, lon_count)
        copies.append(
            pltpu.make_async_remote_copy(
                src_ref=cot_ref.at[there],
                dst_ref=rows_ref.at[:, lon],
                send_sem=cot_send.at[step],
                recv_sem=cot_recv.at[step],
                device_id=(lat, there),
                device_id_type=pl.DeviceIdType.MESH,
            )
        )
    for step in range(1, lat_count):
        there = lax.rem(lat + step, lat_count)
        copies.append(
            pltpu.make_async_remote_copy(
                src_ref=leg_ref.at[there],
                dst_ref=basis_ref.at[lat],
                send_sem=leg_send.at[step],
                recv_sem=leg_recv.at[step],
                device_id=(there, lon),
                device_id_type=pl.DeviceIdType.MESH,
            )
        )
    copies.append(pltpu.make_async_copy(cot_ref.at[lon], rows_ref.at[:, lon], own_sem.at[0]))
    copies.append(pltpu.make_async_copy(leg_ref.at[lat], basis_ref.at[lat], own_sem.at[1]))
    for copy in copies:
        copy.start()
    for copy in copies:
        copy.wait()


def exchange(cotangent, basis, lat_count, lon_count):
    lat_rows, lon_dev, width = cotangent.shape
    rows_each = lat_rows // lon_count
    anywhere = pl.BlockSpec(memory_space=pl.ANY)
    return pl.pallas_call(
        functools.partial(exchange_kernel, lat_count, lon_count),
        out_shape=(
            jax.ShapeDtypeStruct((rows_each, lon_count, lon_dev, width), jnp.bfloat16),
            jax.ShapeDtypeStruct(basis.shape, jnp.bfloat16),
        ),
        in_specs=[anywhere] * 2,
        out_specs=(anywhere, anywhere),
        scratch_shapes=[
            pltpu.SemaphoreType.DMA((lon_count,)),
            pltpu.SemaphoreType.DMA((lon_count,)),
            pltpu.SemaphoreType.DMA((lat_count,)),
            pltpu.SemaphoreType.DMA((lat_count,)),
            pltpu.SemaphoreType.DMA((2,)),
        ],
        compiler_params=pltpu.CompilerParams(collective_id=0, has_side_effects=True),
    )(cotangent.reshape(lon_count, rows_each, lon_dev, width), basis)


MESH = pl.DeviceIdType.MESH


def place_of(index, lon_count):
    return (lax.div(index, lon_count), lax.rem(index, lon_count))


def greet_all(total, me, lon_count):
    barrier = pltpu.get_barrier_semaphore()

    def greet(step, carry):
        there = place_of(lax.rem(me + step, total), lon_count)
        pl.semaphore_signal(barrier, inc=1, device_id=there, device_id_type=MESH)
        return carry

    lax.fori_loop(1, total, greet, 0)
    pl.semaphore_wait(barrier, total - 1)


def forward_kernel(
    lat_count, lon_count, cot_ref, leg_ref, table_ref, coeffs_ref, basis_ref,
    rows, spectra, cot_send, cot_recv, leg_send, leg_recv, all_send, all_recv, own_cot, own_leg,
    own_all,
):
    lat, lon = lax.axis_index("lat"), lax.axis_index("lon")
    total = lat_count * lon_count
    me = lat * lon_count + lon
    row_count = rows.shape[0]
    greet_all(total, me, lon_count)

    def row_copies(row):
        copies = []
        for step in range(1, lon_count):
            there = lax.rem(lon + step, lon_count)
            copies.append(
                pltpu.make_async_remote_copy(
                    src_ref=cot_ref.at[there, row],
                    dst_ref=rows.at[row, lon],
                    send_sem=cot_send.at[row, step],
                    recv_sem=cot_recv.at[row, step],
                    device_id=(lat, there),
                    device_id_type=MESH,
                )
            )
        copies.append(
            pltpu.make_async_copy(cot_ref.at[lon, row], rows.at[row, lon], own_cot.at[row])
        )
        return copies

    def start_row(row):
        for copy in row_copies(row):
            copy.start()

    leg_copies = []
    for step in range(1, lat_count):
        there = lax.rem(lat + step, lat_count)
        leg_copies.append(
            pltpu.make_async_remote_copy(
                src_ref=leg_ref.at[there],
                dst_ref=basis_ref.at[lat],
                send_sem=leg_send.at[step],
                recv_sem=leg_recv.at[step],
                device_id=(there, lon),
                device_id_type=MESH,
            )
        )
    leg_copies.append(pltpu.make_async_copy(leg_ref.at[lat], basis_ref.at[lat], own_leg))

    def all_copy(row, step):
        there = lax.rem(me + step, total)
        return pltpu.make_async_remote_copy(
            src_ref=spectra.at[row, there],
            dst_ref=coeffs_ref.at[me, row],
            send_sem=all_send.at[row, step],
            recv_sem=all_recv.at[row, step],
            device_id=place_of(there, lon_count),
            device_id_type=MESH,
        )

    def own_copy(row):
        return pltpu.make_async_copy(spectra.at[row, me], coeffs_ref.at[me, row], own_all.at[row])

    for row in range(min(2, row_count)):
        start_row(row)
    for copy in leg_copies:
        copy.start()

    def transform(row, carry):
        for copy in row_copies(row):
            copy.wait()

        @pl.when(row + 2 < row_count)
        def _():
            start_row(row + 2)

        value = jnp.dot(table_ref[0], rows[row, 0], preferred_element_type=jnp.float32)
        for block in range(1, lon_count):
            value += jnp.dot(
                table_ref[block], rows[row, block], preferred_element_type=jnp.float32
            )
        spectra[row] = value.reshape(spectra.shape[1:]).astype(jnp.bfloat16)

        def send(step, inner):
            all_copy(row, step).start()
            return inner

        lax.fori_loop(1, total, send, 0)
        own_copy(row).start()
        return carry

    lax.fori_loop(0, row_count, transform, 0)

    def finish(row, carry):
        def arrived(step, inner):
            all_copy(row, step).wait()
            return inner

        lax.fori_loop(1, total, arrived, 0)
        own_copy(row).wait()
        return carry

    lax.fori_loop(0, row_count, finish, 0)
    for copy in leg_copies:
        copy.wait()


def backward_kernel(
    lat_count, lon_count, grads_ref, table_ref, spatial_ref,
    held, stage, all_send, all_recv, lon_send, lon_recv, own_all, own_lon,
):
    lat, lon = lax.axis_index("lat"), lax.axis_index("lon")
    total = lat_count * lon_count
    me = lat * lon_count + lon
    row_count = held.shape[0]
    greet_all(total, me, lon_count)

    def all_copy(row, step):
        there = lax.rem(me + step, total)
        return pltpu.make_async_remote_copy(
            src_ref=grads_ref.at[there, row],
            dst_ref=held.at[row, me],
            send_sem=all_send.at[row, step],
            recv_sem=all_recv.at[row, step],
            device_id=place_of(there, lon_count),
            device_id_type=MESH,
        )

    def own_copy(row):
        return pltpu.make_async_copy(grads_ref.at[me, row], held.at[row, me], own_all.at[row])

    def start_row(row):
        def send(step, inner):
            all_copy(row, step).start()
            return inner

        lax.fori_loop(1, total, send, 0)
        own_copy(row).start()

    def wait_row(row):
        def arrived(step, inner):
            all_copy(row, step).wait()
            return inner

        lax.fori_loop(1, total, arrived, 0)
        own_copy(row).wait()

    def row_copies(row):
        copies = []
        for step in range(1, lon_count):
            there = lax.rem(lon + step, lon_count)
            copies.append(
                pltpu.make_async_remote_copy(
                    src_ref=stage.at[row, there],
                    dst_ref=spatial_ref.at[lon, row],
                    send_sem=lon_send.at[row, step],
                    recv_sem=lon_recv.at[row, step],
                    device_id=(lat, there),
                    device_id_type=MESH,
                )
            )
        copies.append(
            pltpu.make_async_copy(stage.at[row, lon], spatial_ref.at[lon, row], own_lon.at[row])
        )
        return copies

    for row in range(min(2, row_count)):
        start_row(row)

    def transform(row, carry):
        wait_row(row)

        @pl.when(row + 2 < row_count)
        def _():
            start_row(row + 2)

        depth = held.shape[1] * held.shape[2]
        value = held[row].astype(jnp.float32).reshape(depth, -1).astype(jnp.bfloat16)
        for block in range(lon_count):
            stage[row, block] = jnp.dot(
                table_ref[block], value, preferred_element_type=jnp.float32
            ).astype(jnp.bfloat16)
        for copy in row_copies(row):
            copy.start()
        return carry

    lax.fori_loop(0, row_count, transform, 0)

    def finish(row, carry):
        for copy in row_copies(row):
            copy.wait()
        return carry

    lax.fori_loop(0, row_count, finish, 0)


def forward(cotangent, basis, table, lat_count, lon_count, waves):
    lat_rows, lon_dev, width = cotangent.shape
    rows_each, total = lat_rows // lon_count, lat_count * lon_count
    anywhere = pl.BlockSpec(memory_space=pl.ANY)
    dma = pltpu.SemaphoreType.DMA
    blocks = table.reshape(-1, lon_count, lon_dev).transpose(1, 0, 2)
    return pl.pallas_call(
        functools.partial(forward_kernel, lat_count, lon_count),
        out_shape=(
            jax.ShapeDtypeStruct((total, rows_each, waves, width), jnp.bfloat16),
            jax.ShapeDtypeStruct(basis.shape, jnp.bfloat16),
        ),
        in_specs=[anywhere, anywhere, pl.BlockSpec(memory_space=pltpu.VMEM)],
        out_specs=(anywhere, anywhere),
        scratch_shapes=[
            pltpu.VMEM((rows_each, lon_count, lon_dev, width), jnp.bfloat16),
            pltpu.VMEM((rows_each, total, waves, width), jnp.bfloat16),
            dma((rows_each, lon_count)),
            dma((rows_each, lon_count)),
            dma((lat_count,)),
            dma((lat_count,)),
            dma((rows_each, total)),
            dma((rows_each, total)),
            dma((rows_each,)),
            dma,
            dma((rows_each,)),
        ],
        compiler_params=pltpu.CompilerParams(
            collective_id=1, has_side_effects=True, vmem_limit_bytes=40 * 2**20
        ),
    )(cotangent.reshape(lon_count, rows_each, lon_dev, width), basis, jnp.asarray(blocks))


def backward(grads, table, lat_count, lon_count, lon_dev):
    total, rows_each, waves, width = grads.shape
    anywhere = pl.BlockSpec(memory_space=pl.ANY)
    dma = pltpu.SemaphoreType.DMA
    blocks = table.reshape(-1, lon_count, lon_dev).transpose(1, 2, 0)
    return pl.pallas_call(
        functools.partial(backward_kernel, lat_count, lon_count),
        out_shape=jax.ShapeDtypeStruct((lon_count, rows_each, lon_dev, width), jnp.bfloat16),
        in_specs=[anywhere, pl.BlockSpec(memory_space=pltpu.VMEM)],
        out_specs=anywhere,
        scratch_shapes=[
            pltpu.VMEM((rows_each, total, waves, width), jnp.bfloat16),
            pltpu.VMEM((rows_each, lon_count, lon_dev, width), jnp.bfloat16),
            dma((rows_each, total)),
            dma((rows_each, total)),
            dma((rows_each, lon_count)),
            dma((rows_each, lon_count)),
            dma((rows_each,)),
            dma((rows_each,)),
        ],
        compiler_params=pltpu.CompilerParams(
            collective_id=2, has_side_effects=True, vmem_limit_bytes=40 * 2**20
        ),
    )(grads, jnp.asarray(blocks))


def shards(table, cotangent, legendre, spectral_weight, skip_weight):
    lat_rows, lon_dev, width = cotangent.shape
    lat_count = lax.axis_size("lat")
    lon_count = lax.axis_size("lon")
    wave_dev, half_deg = legendre.shape[1:]
    wave_each = -(-wave_dev // lat_count)
    count_lat = lat_rows * lat_count
    half_rows = count_lat // 2
    fourier = jnp.asarray(table)

    padded = jnp.pad(legendre, ((0, 0), (0, wave_each * lat_count - wave_dev), (0, 0)))
    padded = padded.reshape(lat_rows, lat_count, wave_each, half_deg).transpose(1, 2, 0, 3)
    waves = 2 * wave_each
    fused = waves % 8 == 0 and lon_dev % 8 == 0
    if fused:
        coeffs, basis = forward(cotangent, padded, table, lat_count, lon_count, waves)
    else:
        rows, basis = exchange(cotangent, padded, lat_count, lon_count)
        rows = rows.reshape(-1, lon_dev * lon_count, width)
        spectra = jnp.einsum(
            "kl,rlc->rkc", fourier, rows, preferred_element_type=jnp.float32
        ).astype(jnp.bfloat16)
        coeffs = lax.all_to_all(spectra, BOTH, split_axis=1, concat_axis=0, tiled=True)
    coeffs = coeffs.reshape(2, half_rows, 2, wave_each, width)

    wave_start = lax.axis_index("lon") * wave_dev + lax.axis_index("lat") * wave_each
    extent = (2, 1, wave_each, 1, half_deg)
    wavenum = wave_start + lax.broadcasted_iota(jnp.int32, extent, 2)
    degree = 2 * lax.broadcasted_iota(jnp.int32, extent, 4)
    half = lax.broadcasted_iota(jnp.int32, extent, 0)
    parity = wavenum % 2
    degree = degree + jnp.where(half == 0, parity, 1 - parity)
    basis = basis.reshape(2, lat_count // 2, wave_each, lat_rows, half_deg)
    basis = jnp.where(degree >= wavenum, basis, jnp.zeros_like(basis))
    basis = basis.transpose(0, 2, 1, 3, 4).reshape(2, wave_each, half_rows, half_deg)

    wide = coeffs.astype(jnp.float32)
    combined = jnp.stack([wide[0] + wide[1], wide[0] - wide[1]]).astype(jnp.bfloat16)
    sums = jnp.einsum(
        "qmrk,qrpmc->qmkpc", basis, combined, preferred_element_type=jnp.float32
    ).astype(jnp.bfloat16)
    mixed = jnp.einsum(
        "qmkpc,dc->qmkpd", sums, spectral_weight, preferred_element_type=jnp.float32
    ).astype(jnp.bfloat16)
    projected = jnp.einsum(
        "qmrk,qmkpc->qrpmc", basis, mixed, preferred_element_type=jnp.float32
    ).astype(jnp.bfloat16).astype(jnp.float32)
    grads = jnp.stack([projected[0] + projected[1], projected[0] - projected[1]])
    grads = grads.astype(jnp.bfloat16).reshape(count_lat, 2 * wave_each, width)
    if fused:
        grads = grads.reshape(lat_count * lon_count, -1, waves, width)
        spatial = backward(grads, table, lat_count, lon_count, lon_dev)
    else:
        grads = lax.all_to_all(grads, BOTH, split_axis=0, concat_axis=1, tiled=True)
        grid_part = jnp.einsum(
            "kl,rkc->rlc", fourier, grads, preferred_element_type=jnp.float32
        ).astype(jnp.bfloat16)
        grid_part = grid_part.reshape(-1, lon_count, lon_dev, width).transpose(1, 0, 2, 3)
        spatial = lax.all_to_all(grid_part, "lon", split_axis=0, concat_axis=0, tiled=True)
    spatial = spatial.reshape(cotangent.shape)
    skip_term = jnp.dot(
        cotangent.reshape(-1, width), skip_weight.T, preferred_element_type=jnp.float32
    ).reshape(cotangent.shape)
    return (spatial.astype(jnp.float32) + skip_term).astype(jnp.bfloat16)


def solution(mesh):
    lat_count, lon_count = mesh.shape["lat"], mesh.shape["lon"]

    def whole(cotangent, legendre, spectral_weight, skip_weight):
        count_wave = legendre.shape[1]
        wave_each = -(-(count_wave // lon_count) // lat_count)
        table = fourier_table(cotangent.shape[1], count_wave, lat_count, lon_count, wave_each)
        return jax.shard_map(
            functools.partial(shards, table),
            mesh=mesh,
            in_specs=(P("lat", "lon", None), P("lat", "lon", None), P(), P()),
            out_specs=P("lat", "lon", None),
            check_vma=False,
        )(cotangent, legendre, spectral_weight, skip_weight)

    return whole
```
